32 devices in a mesh: ga: 2 (over y), gx: 2 (over core), yz: 8 (over z, x).
Axes of the slice: x: 2, y: 2, z: 4, core: 2. Of those that a mesh axis runs over, the one named last changes fastest.
Arguments:
- tokens: bfloat16 [32, 18432], P(('ga', 'yz'), 'gx'), parts along dimension 0, may hold values from -6 to 6
- gain: float32 [18432], P('gx'), may hold values from 0.5 to 1.5
- w_qkv: bfloat16 [18432, 12800], P('gx', 'yz'), may hold values from -0.046875 to 0.046875
- kv_cache: bfloat16 [32, 512, 512], P(('ga', 'yz', 'gx')), parts along dimension 0, may hold values from -256 to 256
- lengths: int32 [32], P(('ga', 'yz', 'gx')), parts along dimension 0, may hold values from 2 to 512, as said below
- w_out: bfloat16 [12288, 18432], P('gx', 'yz'), may hold values from -0.0546875 to 0.0546875
Outputs:
- attn_out: bfloat16 [32, 18432], P(('ga', 'gx'), 'yz'), parts along dimension 0
The draws below stay inside these ranges and needn't reach their ends.
There are 2 independent parts, one for each index of `ga`. The reference program is written for one: setup_inputs(seed, part) draws one part's arguments, and reference() takes and returns one part's arrays. A program takes and returns all parts, laid end to end along the dimension named above; an argument that names none is the same for every part. Nothing has to cross between parts.
Inputs may be any that keep to these rules, and one draw needn't show every extreme that they name: `lengths`: every sequence holds at least 2 cached positions; some sequence holds exactly 512.
All inputs are finite; a program needn't handle non-finite values.
Results may differ from the reference program's by a relative error of at most 0.012.
The reference program's roundings to bfloat16 on the way count: a program that leaves them out, or rounds other values in their place, can miss the bound.
Values may be sent and summed in bfloat16 or wider, within the bound.
No kernel may reach another device: no remote copies, remote signals or barrier semaphores. Data moves between devices by JAX's collectives and lax.ppermute only.
A program may use at most 128 MiB of HBM per device.

```python
import jax
import jax.numpy as jnp
from jax import lax

D = 18432
HQ = 48
HD = 256
CTX = 512
BATCH = 16
QKV = 12800


def draw_kv_cache(key, part):
    key = jax.random.fold_in(key, 11)
    first = jax.random.fold_in(key, 0)
    base = jnp.clip(jax.random.normal(first, (BATCH, CTX, 2 * HD), jnp.float32), -6.0, 6.0)
    return base.astype(jnp.bfloat16)


def draw_lengths(key, part):
    key = jax.random.fold_in(key, 5)
    first, second, third = jax.random.split(key, 3)
    values = jax.random.randint(first, (BATCH,), 2, CTX + 1)
    longest = jax.random.randint(second, (), 0, BATCH)
    shortest = (longest + jax.random.randint(third, (), 1, BATCH)) % BATCH
    values = values.at[longest].set(CTX)
    values = values.at[shortest].set(2)
    return values.astype(jnp.int32)


def steps_of(own_key, shape, cuts, low, top_value):
    def one(dim, blocks):
        heights = jax.random.uniform(jax.random.fold_in(jax.random.fold_in(own_key, 6), dim), (blocks,), jnp.float32, low / len(cuts), top_value / len(cuts))
        return jnp.repeat(jnp.exp(heights), shape[dim] // blocks).reshape((-1,) + (1,) * (len(shape) - dim - 1))

    factor_of = one(*cuts[0])
    for cut in cuts[1:]:
        factor_of = factor_of * one(*cut)
    return factor_of


def scatter_about(key, shape, width, most, cuts=(), kind=jnp.bfloat16):
    entries = width * jax.random.normal(key, shape, jnp.float32)
    if cuts:
        entries = entries * steps_of(key, shape, cuts, -0.22, 0.18)
    return jnp.clip(entries, -most, most).astype(kind)


def setup_inputs(seed: int = 0, part: int = 0) -> dict:
    key_of = jax.random.split(jax.random.key(seed), 7)
    part_keys = jax.random.split(jax.random.fold_in(key_of[6], part), 7)
    return {
        "tokens": scatter_about(part_keys[0], (BATCH, D), 1.0, 6.0, ((0, 8), (1, 2))),
        "gain": jnp.clip(1.0 + 0.1 * jax.random.normal(key_of[1], (D,), jnp.float32), 0.5, 1.5),
        "w_qkv": scatter_about(key_of[2], (D, QKV), D ** -0.5, 0.046875, ((0, 2), (1, 8))),
        "kv_cache": draw_kv_cache(jax.random.fold_in(jax.random.fold_in(key_of[6], part), 71), part),
        "lengths": draw_lengths(jax.random.fold_in(jax.random.fold_in(key_of[6], part), 71), part),
        "w_out": scatter_about(key_of[5], (HQ * HD, D), (HQ * HD) ** -0.5, 0.0546875, ((0, 2), (1, 8))),
    }


def reference(tokens, gain, w_qkv, kv_cache, lengths, w_out):
    values_f = tokens.astype(jnp.float32)
    mean = lax.optimization_barrier(jnp.sum(values_f, axis=1)) / D
    var = lax.optimization_barrier(jnp.sum(values_f * values_f, axis=1)) / D - mean * mean
    normed = ((values_f - mean[:, None]) * lax.rsqrt(var + 1e-06)[:, None] * gain[None, :]).astype(jnp.bfloat16)
    qkv = jnp.dot(normed, w_qkv, preferred_element_type=jnp.float32).astype(jnp.bfloat16)
    query = qkv[:, :HQ * HD].reshape(BATCH, HQ, HD).astype(jnp.float32)
    key_new = qkv[:, HQ * HD:HQ * HD + HD].astype(jnp.float32)
    value_new = qkv[:, HQ * HD + HD:].astype(jnp.float32)
    keys = kv_cache[:, :, :HD].astype(jnp.float32)
    values = kv_cache[:, :, HD:].astype(jnp.float32)
    scores = jnp.einsum('bhd,bsd->bhs', query, keys) / 16.0
    score_new = jnp.einsum('bhd,bd->bh', query, key_new) / 16.0
    valid = jnp.arange(CTX, dtype=jnp.int32)[None, None, :] < lengths[:, None, None]
    masked = jnp.where(valid, scores, -1e+30)
    top = jnp.maximum(lax.optimization_barrier(jnp.max(masked, axis=2)), score_new)
    expd = jnp.where(valid, jnp.exp(masked - top[:, :, None]), 0.0)
    exp_new = jnp.exp(score_new - top)
    total = lax.optimization_barrier(jnp.sum(expd, axis=2)) + exp_new
    probs = (expd / total[:, :, None]).astype(jnp.bfloat16).astype(jnp.float32)
    prob_new = (exp_new / total).astype(jnp.bfloat16).astype(jnp.float32)
    attended = jnp.einsum('bhs,bsd->bhd', probs, values) + prob_new[:, :, None] * value_new[:, None, :]
    attended = attended.astype(jnp.bfloat16).reshape(BATCH, HQ * HD)
    return jnp.dot(attended, w_out, preferred_element_type=jnp.float32).astype(jnp.bfloat16)
```

```python
import jax
import jax.numpy as jnp
from jax import lax
from jax.sharding import PartitionSpec as P

D = 18432
HQ = 48
HD = 256


def scale_rows(values, sums, gain):
    mean = sums[0] / D
    var = sums[1] / D - mean * mean
    centered = values.astype(jnp.float32) - mean[:, None]
    return (centered * lax.rsqrt(var + 1e-06)[:, None] * gain[None, :]).astype(jnp.bfloat16)


def row_sums(values):
    values_f = values.astype(jnp.float32)
    return (jnp.sum(values_f, axis=1), jnp.sum(values_f * values_f, axis=1))


def attend(qkv, kv_cache, lengths):
    seqs = qkv.shape[0]
    query = qkv[:, : HQ * HD].reshape(seqs, HQ, HD)
    key_new = qkv[:, HQ * HD : HQ * HD + HD]
    value_new = qkv[:, HQ * HD + HD :]
    keys = kv_cache[:, :, :HD]
    values = kv_cache[:, :, HD:]
    scores = jnp.einsum("bhd,bsd->bhs", query, keys, preferred_element_type=jnp.float32) / 16.0
    score_new = jnp.einsum("bhd,bd->bh", query, key_new, preferred_element_type=jnp.float32) / 16.0
    valid = jnp.arange(kv_cache.shape[1], dtype=jnp.int32)[None, None, :] < lengths[:, None, None]
    masked = jnp.where(valid, scores, -1e30)
    top = jnp.maximum(jnp.max(masked, axis=2), score_new)
    expd = jnp.where(valid, jnp.exp(masked - top[:, :, None]), 0.0)
    exp_new = jnp.exp(score_new - top)
    total = jnp.sum(expd, axis=2) + exp_new
    probs = (expd / total[:, :, None]).astype(jnp.bfloat16)
    prob_new = (exp_new / total).astype(jnp.bfloat16)
    attended = jnp.einsum("bhs,bsd->bhd", probs, values, preferred_element_type=jnp.float32)
    attended = (
        attended
        + prob_new.astype(jnp.float32)[:, :, None] * value_new.astype(jnp.float32)[:, None, :]
    )
    return attended.astype(jnp.bfloat16).reshape(seqs, HQ * HD)


def gather_rows(rows, axis, size):
    copies = jnp.broadcast_to(rows[None], (size,) + rows.shape)
    return lax.all_to_all(copies, axis, 0, 0, tiled=True).reshape(-1, rows.shape[-1])


def make_on_device(groups, halves):
    def on_device(tokens, gain, w_qkv, kv_cache, lengths, w_out):
        own = lax.axis_index("gx")
        sums = lax.psum(row_sums(tokens), "gx")
        normed = gather_rows(scale_rows(tokens, sums, gain), "yz", groups)
        partial_qkv = jnp.dot(normed, w_qkv, preferred_element_type=jnp.float32)
        seqs = kv_cache.shape[0]
        sent = partial_qkv.reshape(groups * halves, seqs, -1)
        moved = lax.all_to_all(sent, ("yz", "gx"), 0, 0, tiled=True)
        summed = moved.reshape(groups, halves, seqs, -1).sum(axis=1)
        qkv = summed.astype(jnp.bfloat16).transpose(1, 0, 2).reshape(seqs, -1)
        attended = attend(qkv, kv_cache, lengths)
        by_half = attended.reshape(seqs, halves, -1).transpose(1, 0, 2)
        sent = jnp.broadcast_to(by_half[None], (groups,) + by_half.shape)
        sent = sent.reshape((groups * halves,) + by_half.shape[1:])
        heads = lax.all_to_all(sent, ("yz", "gx"), 0, 0, tiled=True)
        terms = jnp.dot(
            heads.reshape(groups * halves * seqs, -1), w_out, preferred_element_type=jnp.float32
        )
        terms = terms.reshape(halves, -1, terms.shape[1])
        kept = lax.dynamic_index_in_dim(terms, own, 0, keepdims=False)
        given = lax.dynamic_index_in_dim(terms, 1 - own, 0, keepdims=False)
        got = lax.ppermute(given, "gx", [(i, (i + 1) % halves) for i in range(halves)])
        return (kept + got).astype(jnp.bfloat16)

    return on_device


def solution(mesh):
    on_device = make_on_device(mesh.shape["yz"], mesh.shape["gx"])
    placed = (
        P(("ga", "yz"), "gx"),
        P("gx"),
        P("gx", "yz"),
        P(("ga", "yz", "gx"), None, None),
        P(("ga", "yz", "gx")),
        P("gx", "yz"),
    )
    return jax.shard_map(
        on_device, mesh=mesh, in_specs=placed, out_specs=P(("ga", "gx"), "yz"), check_vma=False
    )
```

```python
import functools

import jax
import jax.numpy as jnp
from jax import lax
from jax.experimental import pallas as pl
from jax.experimental.pallas import tpu as pltpu
from jax.sharding import PartitionSpec as P

D = 18432
HQ = 48
HD = 256
MIB = 1 << 20
VMEM = pl.BlockSpec(memory_space=pltpu.VMEM)
ANY = pl.BlockSpec(memory_space=pl.ANY)
SMEM = pl.BlockSpec(memory_space=pltpu.SMEM)


def bytes_of(*shapes):
    total = 0
    for shape, width in shapes:
        size = width
        for dim in shape:
            size *= dim
        total += size
    return total


def spec_of(out):
    return VMEM if isinstance(out, jax.ShapeDtypeStruct) else ANY


def call(kernel, outs, in_specs, scratch, room, cost, *args):
    return pl.pallas_call(
        kernel,
        out_shape=outs,
        in_specs=in_specs,
        out_specs=jax.tree.map(spec_of, outs),
        scratch_shapes=scratch,
        compiler_params=pltpu.CompilerParams(vmem_limit_bytes=room + MIB),
        cost_estimate=pl.CostEstimate(flops=cost[0], bytes_accessed=cost[1], transcendentals=0),
    )(*args)


def sums_kernel(
    lengths_ref, tokens_hbm, gain_hbm, own_ref, gain_ref, sums_ref, used_ref, spare_hbm, own_sem, gain_sem
):
    own_copy = pltpu.make_async_copy(tokens_hbm, own_ref, own_sem)
    gain_copy = pltpu.make_async_copy(gain_hbm, gain_ref, gain_sem)
    own_copy.start()
    gain_copy.start()
    used_ref[...] = jnp.full(used_ref.shape, lengths_ref[0], jnp.int32)
    own_copy.wait()
    own = own_ref[...].astype(jnp.float32)
    lanes = sums_ref.shape[1:]
    sums_ref[0] = jnp.broadcast_to(jnp.sum(own, axis=1, keepdims=True), lanes)
    sums_ref[1] = jnp.broadcast_to(jnp.sum(own * own, axis=1, keepdims=True), lanes)
    gain_copy.wait()


def norm_kernel(own_ref, gain_ref, sums_ref, other_ref, spare_hbm, out_ref):
    total = sums_ref[0][:, 0:1] + other_ref[0][:, 0:1]
    squares = sums_ref[1][:, 0:1] + other_ref[1][:, 0:1]
    mean = total / D
    var = squares / D - mean * mean
    own = own_ref[...].astype(jnp.float32)
    normed = ((own - mean) * lax.rsqrt(var + 1e-06) * gain_ref[...]).astype(jnp.bfloat16)
    for i in range(out_ref.shape[0]):
        out_ref[i] = normed


def project_kernel(rows_ref, weight_ref, spare_hbm, out_ref, wide):
    groups, per, depth = rows_ref.shape
    for i in range(groups):
        wide[i * per : (i + 1) * per, :] = rows_ref[i].astype(jnp.float32)
    rows = wide[...].astype(jnp.bfloat16)
    terms = lax.dot_general(
        rows, weight_ref[...], (((1,), (1,)), ((), ())), preferred_element_type=jnp.float32
    )
    for i in range(out_ref.shape[0]):
        out_ref[i] = terms[i : i + 1, :]


def attend_kernel(halves, used_ref, parts_ref, cache_ref, spare_hbm, out_ref, heads):
    width = parts_ref.shape[2]
    pieces = []
    for i in range(parts_ref.shape[0] // halves):
        piece = parts_ref[i * halves]
        for j in range(1, halves):
            piece = piece + parts_ref[i * halves + j]
        pieces.append(piece)
    for h in range(HQ + 2):
        at = 0
        while at < HD:
            where = h * HD + at
            piece, start = where // width, where % width
            size = min(HD - at, width - start)
            heads[h : h + 1, at : at + size] = pieces[piece][:, start : start + size]
            at += size
    query = heads[0:HQ, :].astype(jnp.bfloat16)
    new = heads[HQ : HQ + 2, :].astype(jnp.bfloat16).astype(jnp.float32)
    cache = cache_ref[0]
    scores = (
        lax.dot_general(
            query, cache[:, :HD], (((1,), (1,)), ((), ())), preferred_element_type=jnp.float32
        )
        / 16.0
    )
    score_new = (
        jnp.sum(query.astype(jnp.float32) * new[0:1, :], axis=1, keepdims=True) / 16.0
    )
    valid = lax.broadcasted_iota(jnp.int32, scores.shape, 1) < used_ref[0:1, 0:1]
    masked = jnp.where(valid, scores, -1e30)
    top = jnp.maximum(jnp.max(masked, axis=1, keepdims=True), score_new)
    expd = jnp.where(valid, jnp.exp(masked - top), 0.0)
    exp_new = jnp.exp(score_new - top)
    total = jnp.sum(expd, axis=1, keepdims=True) + exp_new
    probs = (expd / total).astype(jnp.bfloat16)
    prob_new = (exp_new / total).astype(jnp.bfloat16).astype(jnp.float32)
    attended = jnp.dot(probs, cache[:, HD:], preferred_element_type=jnp.float32)
    attended = (attended + prob_new * new[1:2, :]).astype(jnp.bfloat16)
    per = HQ // halves
    for i in range(out_ref.shape[0]):
        j = i % halves
        out_ref[i] = attended[j * per : (j + 1) * per, :]


def output_kernel(halves, attended_ref, weight_ref, kept_ref, given_ref, wide, rows):
    seqs, per, depth = attended_ref.shape
    lanes = wide.shape[2]
    for c in range(depth // lanes):
        part = attended_ref[:, :, c * lanes : (c + 1) * lanes].astype(jnp.float32)
        wide[c] = part.reshape(seqs * per, lanes)
        for h in range(per):
            at = h * depth + c * lanes
            rows[:, at : at + lanes] = wide[c, pl.ds(h, seqs, stride=per), :].astype(jnp.bfloat16)
    terms = jnp.dot(rows[...], weight_ref[...], preferred_element_type=jnp.float32)
    own = lax.axis_index("gx")
    size = seqs // halves

    @pl.when(own == 0)
    def _():
        kept_ref[...] = terms[:size]
        given_ref[...] = terms[size:]

    @pl.when(own != 0)
    def _():
        kept_ref[...] = terms[size:]
        given_ref[...] = terms[:size]


def make_on_device(groups, halves):
    swap = [(i, (i + 1) % halves) for i in range(halves)]

    def on_device(tokens, gain, w_qkv, kv_cache, lengths, w_out):
        f32, bf16 = jnp.float32, jnp.bfloat16
        members = groups * halves
        per, depth = tokens.shape
        width = w_qkv.shape[1]
        wide_out = w_out.shape[1]
        batch = groups * per
        w_in = pltpu.with_memory_space_constraint(w_qkv.T, pltpu.VMEM)
        w_back = pltpu.with_memory_space_constraint(w_out, pltpu.VMEM)

        own, scale, sums, used, spare = call(
            sums_kernel,
            [
                jax.ShapeDtypeStruct((per, depth), bf16),
                jax.ShapeDtypeStruct((1, depth), f32),
                jax.ShapeDtypeStruct((2, per, 128), f32),
                jax.ShapeDtypeStruct((8, 128), jnp.int32),
                pltpu.HBM((2 * depth * width // 1024, 1024), bf16),
            ],
            [SMEM, ANY, ANY],
            [pltpu.SemaphoreType.DMA, pltpu.SemaphoreType.DMA],
            bytes_of(((8, depth), 12)),
            (4 * per * depth, 2 * per * depth),
            lengths,
            pltpu.with_memory_space_constraint(tokens, pltpu.HBM),
            pltpu.with_memory_space_constraint(gain.reshape(1, -1), pltpu.HBM),
        )
        spare = pltpu.with_memory_space_constraint(spare, pltpu.HBM)
        other = lax.ppermute(sums, "gx", swap)
        normed = call(
            norm_kernel,
            jax.ShapeDtypeStruct((groups, per, depth), bf16),
            [VMEM, VMEM, VMEM, VMEM, ANY],
            [],
            bytes_of(((groups, per, depth), 2), ((8, depth), 12)),
            (6 * per * depth, 2 * groups * per * depth),
            own,
            scale,
            sums,
            other,
            spare,
        )
        rows = lax.all_to_all(normed, "yz", 0, 0, tiled=True)
        parts = call(
            project_kernel,
            jax.ShapeDtypeStruct((members, 1, width), f32),
            [VMEM, VMEM, ANY],
            [pltpu.VMEM((batch, depth), f32)],
            bytes_of(((batch, depth), 8), ((batch, width + 128), 16)),
            (2 * batch * depth * width, depth * width * 2),
            rows,
            w_in,
            spare,
        )
        moved = lax.all_to_all(parts, ("yz", "gx"), 0, 0, tiled=True)
        attended = call(
            functools.partial(attend_kernel, halves),
            jax.ShapeDtypeStruct((members, HQ // halves, HD), bf16),
            [VMEM, VMEM, VMEM, ANY],
            [pltpu.VMEM((HQ + 8, HD), f32)],
            bytes_of(((members, HQ // halves, HD), 4), ((512, 512), 4), ((members, 8, width + 128), 8)),
            (4 * HQ * 512 * HD, w_out.shape[0] * wide_out * 2),
            used,
            moved,
            kv_cache,
            spare,
        )
        gathered = lax.all_to_all(attended, ("yz", "gx"), 0, 0, tiled=True)
        size = batch // halves
        kept, given = call(
            functools.partial(output_kernel, halves),
            [jax.ShapeDtypeStruct((size, wide_out), f32)] * 2,
            [VMEM, VMEM],
            [
                pltpu.VMEM((HD // 128, batch * (HQ // halves), 128), f32),
                pltpu.VMEM((batch, HQ // halves * HD), bf16),
            ],
            bytes_of(((batch, HQ // halves, HD), 10), ((batch, wide_out + 128), 12)),
            (2 * batch * w_out.shape[0] * wide_out, w_out.shape[0] * wide_out * 2),
            gathered,
            w_back,
        )
        got = lax.ppermute(given, "gx", swap)
        return (kept + got).astype(bf16)

    return on_device


def solution(mesh):
    placed = (
        P(("ga", "yz"), "gx"),
        P("gx"),
        P("gx", "yz"),
        P(("ga", "yz", "gx"), None, None),
        P(("ga", "yz", "gx")),
        P("gx", "yz"),
    )
    return jax.shard_map(
        make_on_device(mesh.shape["yz"], mesh.shape["gx"]),
        mesh=mesh,
        in_specs=placed,
        out_specs=P(("ga", "gx"), "yz"),
        check_vma=False,
    )
```

```python
import functools

import jax
import jax.numpy as jnp
from jax import lax
from jax.experimental import pallas as pl
from jax.experimental.pallas import tpu as pltpu
from jax.sharding import PartitionSpec as P

D = 18432
HQ = 48
HD = 256
MIB = 1 << 20
VMEM = pl.BlockSpec(memory_space=pltpu.VMEM)
SMEM = pl.BlockSpec(memory_space=pltpu.SMEM)
ANY = pl.BlockSpec(memory_space=pl.ANY)


def bytes_of(*shapes):
    total = 0
    for shape, width in shapes:
        size = width
        for dim in shape:
            size *= dim
        total += size
    return total


def spec_of(out):
    return VMEM if isinstance(out, jax.ShapeDtypeStruct) else ANY


def call(kernel, outs, in_specs, scratch, room, cost, *args):
    return pl.pallas_call(
        kernel,
        out_shape=outs,
        in_specs=in_specs,
        out_specs=jax.tree.map(spec_of, outs),
        scratch_shapes=scratch,
        compiler_params=pltpu.CompilerParams(vmem_limit_bytes=room + MIB),
        cost_estimate=pl.CostEstimate(flops=cost[0], bytes_accessed=cost[1], transcendentals=0),
    )(*args)


def load_kernel(
    lengths_ref, tokens_hbm, gain_hbm, own_ref, gain_ref, used_ref, spare_hbm, sems
):
    copies = [
        pltpu.make_async_copy(tokens_hbm, own_ref, sems.at[0]),
        pltpu.make_async_copy(gain_hbm, gain_ref, sems.at[1]),
    ]
    for copy in copies:
        copy.start()
    used_ref[...] = jnp.full(used_ref.shape, lengths_ref[0], jnp.int32)
    for copy in copies:
        copy.wait()


def sums_kernel(rows_refs, sums_ref):
    for i, ref in enumerate(rows_refs):
        rows = ref[...].astype(jnp.float32)
        lanes = sums_ref.shape[2:]
        sums_ref[i, 0] = jnp.broadcast_to(jnp.sum(rows, axis=1, keepdims=True), lanes)
        sums_ref[i, 1] = jnp.broadcast_to(jnp.sum(rows * rows, axis=1, keepdims=True), lanes)


def norm_kernel(rows_refs, gain_ref, sums_ref, other_ref, spare_hbm, out_ref):
    for i, ref in enumerate(rows_refs):
        total = sums_ref[i, 0][:, 0:1] + other_ref[i, 0][:, 0:1]
        squares = sums_ref[i, 1][:, 0:1] + other_ref[i, 1][:, 0:1]
        mean = total / D
        var = squares / D - mean * mean
        rows = ref[...].astype(jnp.float32)
        normed = ((rows - mean) * lax.rsqrt(var + 1e-06) * gain_ref[...]).astype(jnp.bfloat16)
        out_ref[i] = normed


def project_kernel(order, block_refs, weight_ref, out_ref, wide):
    group = lax.axis_index("yz")
    at, places = 0, []
    for ref, origins in zip(block_refs, order):
        per = ref.shape[1]
        for i, origin in enumerate(origins):
            wide[at : at + per, :] = ref[i].astype(jnp.float32)
            places.extend(origin(group) * per + r for r in range(per))
            at += per
    rows = wide[...].astype(jnp.bfloat16)
    terms = lax.dot_general(
        rows, weight_ref[...], (((1,), (1,)), ((), ())), preferred_element_type=jnp.float32
    )
    for i, place in enumerate(places):
        out_ref[place] = terms[i : i + 1, :]


def attend_kernel(halves, used_ref, parts_ref, cache_ref, spare_refs, out_ref, heads):
    width = parts_ref.shape[2]
    pieces = []
    for i in range(parts_ref.shape[0] // halves):
        piece = parts_ref[i * halves]
        for j in range(1, halves):
            piece = piece + parts_ref[i * halves + j]
        pieces.append(piece)
    for h in range(HQ + 2):
        at = 0
        while at < HD:
            where = h * HD + at
            piece, start = where // width, where % width
            size = min(HD - at, width - start)
            heads[h : h + 1, at : at + size] = pieces[piece][:, start : start + size]
            at += size
    query = heads[0:HQ, :].astype(jnp.bfloat16)
    new = heads[HQ : HQ + 2, :].astype(jnp.bfloat16).astype(jnp.float32)
    cache = cache_ref[0]
    scores = (
        lax.dot_general(
            query, cache[:, :HD], (((1,), (1,)), ((), ())), preferred_element_type=jnp.float32
        )
        / 16.0
    )
    score_new = (
        jnp.sum(query.astype(jnp.float32) * new[0:1, :], axis=1, keepdims=True) / 16.0
    )
    valid = lax.broadcasted_iota(jnp.int32, scores.shape, 1) < used_ref[0:1, 0:1]
    masked = jnp.where(valid, scores, -1e30)
    top = jnp.maximum(jnp.max(masked, axis=1, keepdims=True), score_new)
    expd = jnp.where(valid, jnp.exp(masked - top), 0.0)
    exp_new = jnp.exp(score_new - top)
    total = jnp.sum(expd, axis=1, keepdims=True) + exp_new
    probs = (expd / total).astype(jnp.bfloat16)
    prob_new = (exp_new / total).astype(jnp.bfloat16).astype(jnp.float32)
    attended = jnp.dot(probs, cache[:, HD:], preferred_element_type=jnp.float32)
    attended = (attended + prob_new * new[1:2, :]).astype(jnp.bfloat16)
    per = HQ // halves
    for i in range(out_ref.shape[0]):
        j = i % halves
        out_ref[i] = attended[j * per : (j + 1) * per, :]


def output_kernel(halves, attended_ref, weight_ref, kept_ref, given_ref, wide, rows):
    seqs, per, depth = attended_ref.shape
    lanes = wide.shape[2]
    for c in range(depth // lanes):
        part = attended_ref[:, :, c * lanes : (c + 1) * lanes].astype(jnp.float32)
        wide[c] = part.reshape(seqs * per, lanes)
        for h in range(per):
            at = h * depth + c * lanes
            rows[:, at : at + lanes] = wide[c, pl.ds(h, seqs, stride=per), :].astype(jnp.bfloat16)
    terms = jnp.dot(rows[...], weight_ref[...], preferred_element_type=jnp.float32)
    own = lax.axis_index("gx")
    size = seqs // halves

    @pl.when(own == 0)
    def _():
        kept_ref[...] = terms[:size]
        given_ref[...] = terms[size:]

    @pl.when(own != 0)
    def _():
        kept_ref[...] = terms[size:]
        given_ref[...] = terms[:size]


def make_on_device(groups, halves):
    swap = [(i, (i + 1) % halves) for i in range(halves)]

    def pairs(k):
        return [(i, i ^ k) for i in range(groups)]

    def on_device(tokens, gain, w_qkv, kv_cache, lengths, w_out):
        f32, bf16 = jnp.float32, jnp.bfloat16
        members = groups * halves
        per, depth = tokens.shape
        width = w_qkv.shape[1]
        wide_out = w_out.shape[1]
        batch = groups * per
        w_in = pltpu.with_memory_space_constraint(w_qkv.T, pltpu.VMEM)
        w_back = pltpu.with_memory_space_constraint(w_out, pltpu.VMEM)

        own, scale, used, spare = call(
            load_kernel,
            [
                jax.ShapeDtypeStruct((per, depth), bf16),
                jax.ShapeDtypeStruct((1, depth), f32),
                jax.ShapeDtypeStruct((8, 128), jnp.int32),
                pltpu.HBM((2 * depth * width // 1024, 1024), bf16),
            ],
            [SMEM, ANY, ANY],
            [pltpu.SemaphoreType.DMA((2,))],
            bytes_of(((8, depth), 8)),
            (per * depth, 2 * per * depth),
            lengths,
            pltpu.with_memory_space_constraint(tokens, pltpu.HBM),
            pltpu.with_memory_space_constraint(gain.reshape(1, -1), pltpu.HBM),
        )
        spare = pltpu.with_memory_space_constraint(spare, pltpu.HBM)
        mate = lax.ppermute(tokens, "yz", pairs(1))
        sums = call(
            sums_kernel,
            jax.ShapeDtypeStruct((2, 2, per, 128), f32),
            [[VMEM, VMEM]],
            [],
            bytes_of(((8, depth), 8)),
            (8 * per * depth, 4 * per * depth),
            [own, mate],
        )
        other = lax.ppermute(sums, "gx", swap)
        normed = call(
            norm_kernel,
            jax.ShapeDtypeStruct((2, per, depth), bf16),
            [[VMEM, VMEM], VMEM, VMEM, VMEM, ANY],
            [],
            bytes_of(((8, depth), 24)),
            (12 * per * depth, 4 * per * depth),
            [own, mate],
            scale,
            sums,
            other,
            spare,
        )
        blocks = [normed] + [lax.ppermute(normed, "yz", pairs(k)) for k in range(2, groups, 2)]
        order = [
            [lambda g, k=k: g ^ k, lambda g, k=k: g ^ k ^ 1] for k in range(0, groups, 2)
        ]
        parts = call(
            functools.partial(project_kernel, order),
            jax.ShapeDtypeStruct((members, 1, width), f32),
            [[VMEM] * len(blocks), VMEM],
            [pltpu.VMEM((batch, depth), f32)],
            bytes_of(((batch, depth), 8), ((batch, width + 128), 16)),
            (2 * batch * depth * width, depth * width * 2),
            blocks,
            w_in,
        )
        moved = lax.all_to_all(parts, ("yz", "gx"), 0, 0, tiled=True)
        attended = call(
            functools.partial(attend_kernel, halves),
            jax.ShapeDtypeStruct((members, HQ // halves, HD), bf16),
            [VMEM, VMEM, VMEM, [ANY] * 4],
            [pltpu.VMEM((HQ + 8, HD), f32)],
            bytes_of(((members, HQ // halves, HD), 4), ((512, 512), 4), ((members, 8, width + 128), 8)),
            (4 * HQ * 512 * HD, w_out.shape[0] * wide_out * 2),
            used,
            moved,
            kv_cache,
            [spare] * 4,
        )
        gathered = lax.all_to_all(attended, ("yz", "gx"), 0, 0, tiled=True)
        size = batch // halves
        kept, given = call(
            functools.partial(output_kernel, halves),
            [jax.ShapeDtypeStruct((size, wide_out), f32)] * 2,
            [VMEM, VMEM],
            [
                pltpu.VMEM((HD // 128, batch * (HQ // halves), 128), f32),
                pltpu.VMEM((batch, HQ // halves * HD), bf16),
            ],
            bytes_of(((batch, HQ // halves, HD), 10), ((batch, wide_out + 128), 12)),
            (2 * batch * w_out.shape[0] * wide_out, w_out.shape[0] * wide_out * 2),
            gathered,
            w_back,
        )
        got = lax.ppermute(given, "gx", swap)
        return (kept + got).astype(bf16)

    return on_device


def solution(mesh):
    placed = (
        P(("ga", "yz"), "gx"),
        P("gx"),
        P("gx", "yz"),
        P(("ga", "yz", "gx"), None, None),
        P(("ga", "yz", "gx")),
        P("gx", "yz"),
    )
    return jax.shard_map(
        make_on_device(mesh.shape["yz"], mesh.shape["gx"]),
        mesh=mesh,
        in_specs=placed,
        out_specs=P(("ga", "gx"), "yz"),
        check_vma=False,
    )
```

```python
import functools

import jax
import jax.numpy as jnp
from jax import lax
from jax.experimental import pallas as pl
from jax.experimental.pallas import tpu as pltpu
from jax.sharding import PartitionSpec as P

D = 18432
HQ = 48
HD = 256
BLOCK = 256
MIB = 1 << 20
VMEM = pl.BlockSpec(memory_space=pltpu.VMEM)
SMEM = pl.BlockSpec(memory_space=pltpu.SMEM)
ANY = pl.BlockSpec(memory_space=pl.ANY)


def bytes_of(*shapes):
    total = 0
    for shape, width in shapes:
        size = width
        for dim in shape:
            size *= dim
        total += size
    return total


def spec_of(out):
    return VMEM if isinstance(out, jax.ShapeDtypeStruct) else ANY


def call(kernel, outs, in_specs, scratch, room, cost, *args):
    return pl.pallas_call(
        kernel,
        out_shape=outs,
        in_specs=in_specs,
        out_specs=jax.tree.map(spec_of, outs),
        scratch_shapes=scratch,
        compiler_params=pltpu.CompilerParams(vmem_limit_bytes=room + MIB),
        cost_estimate=pl.CostEstimate(flops=cost[0], bytes_accessed=cost[1], transcendentals=0),
    )(*args)


def load_kernel(
    lengths_ref, tokens_hbm, gain_hbm, own_ref, gain_ref, used_ref, spare_hbm, sems
):
    copies = [
        pltpu.make_async_copy(tokens_hbm, own_ref, sems.at[0]),
        pltpu.make_async_copy(gain_hbm, gain_ref, sems.at[1]),
    ]
    for copy in copies:
        copy.start()
    used_ref[...] = jnp.full(used_ref.shape, lengths_ref[0], jnp.int32)
    for copy in copies:
        copy.wait()


def sums_kernel(rows_refs, sums_ref):
    for i, ref in enumerate(rows_refs):
        rows = ref[...].astype(jnp.float32)
        lanes = sums_ref.shape[2:]
        sums_ref[i, 0] = jnp.broadcast_to(jnp.sum(rows, axis=1, keepdims=True), lanes)
        sums_ref[i, 1] = jnp.broadcast_to(jnp.sum(rows * rows, axis=1, keepdims=True), lanes)


def norm_kernel(rows_refs, gain_ref, sums_ref, other_ref, spare_hbm, out_ref):
    for i, ref in enumerate(rows_refs):
        total = sums_ref[i, 0][:, 0:1] + other_ref[i, 0][:, 0:1]
        squares = sums_ref[i, 1][:, 0:1] + other_ref[i, 1][:, 0:1]
        mean = total / D
        var = squares / D - mean * mean
        rows = ref[...].astype(jnp.float32)
        normed = ((rows - mean) * lax.rsqrt(var + 1e-06) * gain_ref[...]).astype(jnp.bfloat16)
        out_ref[i] = normed


def dot_last(left, right):
    return lax.dot_general(
        left, right, (((1,), (1,)), ((), ())), preferred_element_type=jnp.float32
    )


def project_kernel(order, block_refs, weight_ref, out_ref, wide, rows, terms):
    group = lax.axis_index("yz")
    at, places = 0, []
    for ref, origins in zip(block_refs, order):
        per = ref.shape[1]
        for i, origin in enumerate(origins):
            wide[at : at + per, :] = ref[i].astype(jnp.float32)
            places.extend(origin(group) * per + r for r in range(per))
            at += per
    rows[...] = wide[...].astype(jnp.bfloat16)
    batch, depth = rows.shape
    width = weight_ref.shape[0]
    at = 0
    while width - at >= 2 * BLOCK:
        middle, end = at + BLOCK, at + 2 * BLOCK
        first = jnp.zeros((batch, BLOCK), jnp.float32)
        second = jnp.zeros((BLOCK, batch), jnp.float32)
        for k in range(0, depth, BLOCK):
            some = rows[:, k : k + BLOCK]
            second = second + dot_last(weight_ref[middle:end, k : k + BLOCK], some)
            first = first + dot_last(some, weight_ref[at:middle, k : k + BLOCK])
        terms[:, at:middle] = first
        terms[:, middle:end] = second.T
        at = end
    if at < width:
        terms[:, at:] = dot_last(rows[...], weight_ref[at:, :])
    for i, place in enumerate(places):
        out_ref[place] = terms[i : i + 1, :]


def attend_kernel(halves, used_ref, parts_ref, cache_ref, spare_refs, out_ref, heads):
    width = parts_ref.shape[2]
    pieces = []
    for i in range(parts_ref.shape[0] // halves):
        piece = parts_ref[i * halves]
        for j in range(1, halves):
            piece = piece + parts_ref[i * halves + j]
        pieces.append(piece)
    for h in range(HQ + 2):
        at = 0
        while at < HD:
            where = h * HD + at
            piece, start = where // width, where % width
            size = min(HD - at, width - start)
            heads[h : h + 1, at : at + size] = pieces[piece][:, start : start + size]
            at += size
    query = heads[0:HQ, :].astype(jnp.bfloat16)
    new = heads[HQ : HQ + 2, :].astype(jnp.bfloat16).astype(jnp.float32)
    cache = cache_ref[0]
    scores = (
        lax.dot_general(
            query, cache[:, :HD], (((1,), (1,)), ((), ())), preferred_element_type=jnp.float32
        )
        / 16.0
    )
    score_new = (
        jnp.sum(query.astype(jnp.float32) * new[0:1, :], axis=1, keepdims=True) / 16.0
    )
    valid = lax.broadcasted_iota(jnp.int32, scores.shape, 1) < used_ref[0:1, 0:1]
    masked = jnp.where(valid, scores, -1e30)
    top = jnp.maximum(jnp.max(masked, axis=1, keepdims=True), score_new)
    expd = jnp.where(valid, jnp.exp(masked - top), 0.0)
    exp_new = jnp.exp(score_new - top)
    total = jnp.sum(expd, axis=1, keepdims=True) + exp_new
    probs = (expd / total).astype(jnp.bfloat16)
    prob_new = (exp_new / total).astype(jnp.bfloat16).astype(jnp.float32)
    attended = jnp.dot(probs, cache[:, HD:], preferred_element_type=jnp.float32)
    attended = (attended + prob_new * new[1:2, :]).astype(jnp.bfloat16)
    per = HQ // halves
    for i in range(out_ref.shape[0]):
        j = i % halves
        out_ref[i] = attended[j * per : (j + 1) * per, :]


def output_kernel(halves, attended_ref, weight_ref, kept_ref, given_ref, wide, rows):
    seqs, per, depth = attended_ref.shape
    lanes = wide.shape[2]
    for c in range(depth // lanes):
        part = attended_ref[:, :, c * lanes : (c + 1) * lanes].astype(jnp.float32)
        wide[c] = part.reshape(seqs * per, lanes)
        for h in range(per):
            at = h * depth + c * lanes
            rows[:, at : at + lanes] = wide[c, pl.ds(h, seqs, stride=per), :].astype(jnp.bfloat16)
    terms = jnp.dot(rows[...], weight_ref[...], preferred_element_type=jnp.float32)
    own = lax.axis_index("gx")
    size = seqs // halves

    @pl.when(own == 0)
    def _():
        kept_ref[...] = terms[:size]
        given_ref[...] = terms[size:]

    @pl.when(own != 0)
    def _():
        kept_ref[...] = terms[size:]
        given_ref[...] = terms[:size]


def make_on_device(groups, halves):
    swap = [(i, (i + 1) % halves) for i in range(halves)]

    def pairs(k):
        return [(i, i ^ k) for i in range(groups)]

    def on_device(tokens, gain, w_qkv, kv_cache, lengths, w_out):
        f32, bf16 = jnp.float32, jnp.bfloat16
        members = groups * halves
        per, depth = tokens.shape
        width = w_qkv.shape[1]
        wide_out = w_out.shape[1]
        batch = groups * per
        w_in = pltpu.with_memory_space_constraint(w_qkv.T, pltpu.VMEM)
        w_back = pltpu.with_memory_space_constraint(w_out, pltpu.VMEM)

        own, scale, used, spare = call(
            load_kernel,
            [
                jax.ShapeDtypeStruct((per, depth), bf16),
                jax.ShapeDtypeStruct((1, depth), f32),
                jax.ShapeDtypeStruct((8, 128), jnp.int32),
                pltpu.HBM((2 * depth * width // 1024, 1024), bf16),
            ],
            [SMEM, ANY, ANY],
            [pltpu.SemaphoreType.DMA((2,))],
            bytes_of(((8, depth), 8)),
            (per * depth, 2 * per * depth),
            lengths,
            pltpu.with_memory_space_constraint(tokens, pltpu.HBM),
            pltpu.with_memory_space_constraint(gain.reshape(1, -1), pltpu.HBM),
        )
        spare = pltpu.with_memory_space_constraint(spare, pltpu.HBM)
        mate = lax.ppermute(tokens, "yz", pairs(1))
        sums = call(
            sums_kernel,
            jax.ShapeDtypeStruct((2, 2, per, 128), f32),
            [[VMEM, VMEM]],
            [],
            bytes_of(((8, depth), 8)),
            (8 * per * depth, 4 * per * depth),
            [own, mate],
        )
        other = lax.ppermute(sums, "gx", swap)
        normed = call(
            norm_kernel,
            jax.ShapeDtypeStruct((2, per, depth), bf16),
            [[VMEM, VMEM], VMEM, VMEM, VMEM, ANY],
            [],
            bytes_of(((8, depth), 24)),
            (12 * per * depth, 4 * per * depth),
            [own, mate],
            scale,
            sums,
            other,
            spare,
        )
        blocks = [normed] + [lax.ppermute(normed, "yz", pairs(k)) for k in range(2, groups, 2)]
        order = [
            [lambda g, k=k: g ^ k, lambda g, k=k: g ^ k ^ 1] for k in range(0, groups, 2)
        ]
        parts = call(
            functools.partial(project_kernel, order),
            jax.ShapeDtypeStruct((members, 1, width), f32),
            [[VMEM] * len(blocks), VMEM],
            [
                pltpu.VMEM((batch, depth), f32),
                pltpu.VMEM((batch, depth), bf16),
                pltpu.VMEM((batch, width), f32),
            ],
            bytes_of(((batch, depth), 8), ((batch, width + 128), 16), ((BLOCK, BLOCK), 8)),
            (2 * batch * depth * width, depth * width * 2),
            blocks,
            w_in,
        )
        moved = lax.all_to_all(parts, ("yz", "gx"), 0, 0, tiled=True)
        attended = call(
            functools.partial(attend_kernel, halves),
            jax.ShapeDtypeStruct((members, HQ // halves, HD), bf16),
            [VMEM, VMEM, VMEM, [ANY] * 4],
            [pltpu.VMEM((HQ + 8, HD), f32)],
            bytes_of(((members, HQ // halves, HD), 4), ((512, 512), 4), ((members, 8, width + 128), 8)),
            (4 * HQ * 512 * HD, w_out.shape[0] * wide_out * 2),
            used,
            moved,
            kv_cache,
            [spare] * 4,
        )
        gathered = lax.all_to_all(attended, ("yz", "gx"), 0, 0, tiled=True)
        size = batch // halves
        kept, given = call(
            functools.partial(output_kernel, halves),
            [jax.ShapeDtypeStruct((size, wide_out), f32)] * 2,
            [VMEM, VMEM],
            [
                pltpu.VMEM((HD // 128, batch * (HQ // halves), 128), f32),
                pltpu.VMEM((batch, HQ // halves * HD), bf16),
            ],
            bytes_of(((batch, HQ // halves, HD), 10), ((batch, wide_out + 128), 12)),
            (2 * batch * w_out.shape[0] * wide_out, w_out.shape[0] * wide_out * 2),
            gathered,
            w_back,
        )
        got = lax.ppermute(given, "gx", swap)
        return (kept + got).astype(bf16)

    return on_device


def solution(mesh):
    placed = (
        P(("ga", "yz"), "gx"),
        P("gx"),
        P("gx", "yz"),
        P(("ga", "yz", "gx"), None, None),
        P(("ga", "yz", "gx")),
        P("gx", "yz"),
    )
    return jax.shard_map(
        make_on_device(mesh.shape["yz"], mesh.shape["gx"]),
        mesh=mesh,
        in_specs=placed,
        out_specs=P(("ga", "gx"), "yz"),
        check_vma=False,
    )
```

```python
import functools

import jax
import jax.numpy as jnp
from jax import lax
from jax.experimental import pallas as pl
from jax.experimental.pallas import tpu as pltpu
from jax.sharding import PartitionSpec as P

D = 18432
HQ = 48
HD = 256
BLOCK = 256
MIB = 1 << 20
VMEM = pl.BlockSpec(memory_space=pltpu.VMEM)
SMEM = pl.BlockSpec(memory_space=pltpu.SMEM)
ANY = pl.BlockSpec(memory_space=pl.ANY)


def bytes_of(*shapes):
    total = 0
    for shape, width in shapes:
        size = width
        for dim in shape:
            size *= dim
        total += size
    return total


def spec_of(out):
    return VMEM if isinstance(out, jax.ShapeDtypeStruct) else ANY


def call(kernel, outs, in_specs, scratch, room, cost, *args):
    return pl.pallas_call(
        kernel,
        out_shape=outs,
        in_specs=in_specs,
        out_specs=jax.tree.map(spec_of, outs),
        scratch_shapes=scratch,
        compiler_params=pltpu.CompilerParams(vmem_limit_bytes=room + MIB),
        cost_estimate=pl.CostEstimate(flops=cost[0], bytes_accessed=cost[1], transcendentals=0),
    )(*args)


def load_kernel(
    lengths_ref, tokens_hbm, gain_hbm, own_ref, gain_ref, used_ref, spare_hbm, sems
):
    copies = [
        pltpu.make_async_copy(tokens_hbm, own_ref, sems.at[0]),
        pltpu.make_async_copy(gain_hbm, gain_ref, sems.at[1]),
    ]
    for copy in copies:
        copy.start()
    used_ref[...] = jnp.full(used_ref.shape, lengths_ref[0], jnp.int32)
    for copy in copies:
        copy.wait()


def column_kernel(rows_refs, spare_hbm, column_ref, sums_ref):
    lanes = sums_ref.shape[2:]
    for i, ref in enumerate(rows_refs):
        column_ref[i] = ref[...]
        rows = ref[...].astype(jnp.float32)
        sums_ref[i, 0] = jnp.broadcast_to(jnp.sum(rows, axis=1, keepdims=True), lanes)
        sums_ref[i, 1] = jnp.broadcast_to(jnp.sum(rows * rows, axis=1, keepdims=True), lanes)


def stats_kernel(sums_ref, other_ref, stats_ref):
    for i in range(sums_ref.shape[0]):
        mean = (sums_ref[i, 0] + other_ref[i, 0]) / D
        var = (sums_ref[i, 1] + other_ref[i, 1]) / D - mean * mean
        stats_ref[i, 0] = mean
        stats_ref[i, 1] = lax.rsqrt(var + 1e-06)


def dot_last(left, right):
    return lax.dot_general(
        left, right, (((1,), (1,)), ((), ())), preferred_element_type=jnp.float32
    )


def project_kernel(
    order, block_refs, stats_refs, gain_ref, weight_ref, out_ref, wide, stats, rows, terms
):
    group = lax.axis_index("yz")
    at, places = 0, []
    for ref, stats_ref, origins in zip(block_refs, stats_refs, order):
        per = ref.shape[1]
        for i, origin in enumerate(origins):
            wide[at : at + per, :] = ref[i].astype(jnp.float32)
            stats[0, at : at + per, :] = stats_ref[i, 0]
            stats[1, at : at + per, :] = stats_ref[i, 1]
            places.extend(origin(group) * per + r for r in range(per))
            at += per
    mean, scale = stats[0][:, 0:1], stats[1][:, 0:1]
    rows[...] = ((wide[...] - mean) * scale * gain_ref[...]).astype(jnp.bfloat16)
    batch, depth = rows.shape
    width = weight_ref.shape[0]
    at = 0
    while width - at >= 2 * BLOCK:
        middle, end = at + BLOCK, at + 2 * BLOCK
        first = jnp.zeros((batch, BLOCK), jnp.float32)
        second = jnp.zeros((BLOCK, batch), jnp.float32)
        for k in range(0, depth, BLOCK):
            some = rows[:, k : k + BLOCK]
            second = second + dot_last(weight_ref[middle:end, k : k + BLOCK], some)
            first = first + dot_last(some, weight_ref[at:middle, k : k + BLOCK])
        terms[:, at:middle] = first
        terms[:, middle:end] = second.T
        at = end
    if at < width:
        terms[:, at:] = dot_last(rows[...], weight_ref[at:, :])
    for i, place in enumerate(places):
        out_ref[place] = terms[i : i + 1, :]


def attend_kernel(halves, used_ref, parts_ref, cache_ref, spare_refs, out_ref, heads):
    width = parts_ref.shape[2]
    pieces = []
    for i in range(parts_ref.shape[0] // halves):
        piece = parts_ref[i * halves]
        for j in range(1, halves):
            piece = piece + parts_ref[i * halves + j]
        pieces.append(piece)
    for h in range(HQ + 2):
        at = 0
        while at < HD:
            where = h * HD + at
            piece, start = where // width, where % width
            size = min(HD - at, width - start)
            heads[h : h + 1, at : at + size] = pieces[piece][:, start : start + size]
            at += size
    query = heads[0:HQ, :].astype(jnp.bfloat16)
    new = heads[HQ : HQ + 2, :].astype(jnp.bfloat16).astype(jnp.float32)
    cache = cache_ref[0]
    scores = (
        lax.dot_general(
            query, cache[:, :HD], (((1,), (1,)), ((), ())), preferred_element_type=jnp.float32
        )
        / 16.0
    )
    score_new = (
        jnp.sum(query.astype(jnp.float32) * new[0:1, :], axis=1, keepdims=True) / 16.0
    )
    valid = lax.broadcasted_iota(jnp.int32, scores.shape, 1) < used_ref[0:1, 0:1]
    masked = jnp.where(valid, scores, -1e30)
    top = jnp.maximum(jnp.max(masked, axis=1, keepdims=True), score_new)
    expd = jnp.where(valid, jnp.exp(masked - top), 0.0)
    exp_new = jnp.exp(score_new - top)
    total = jnp.sum(expd, axis=1, keepdims=True) + exp_new
    probs = (expd / total).astype(jnp.bfloat16)
    prob_new = (exp_new / total).astype(jnp.bfloat16).astype(jnp.float32)
    attended = jnp.dot(probs, cache[:, HD:], preferred_element_type=jnp.float32)
    attended = (attended + prob_new * new[1:2, :]).astype(jnp.bfloat16)
    per = HQ // halves
    for i in range(out_ref.shape[0]):
        j = i % halves
        out_ref[i] = attended[j * per : (j + 1) * per, :]


def output_kernel(halves, attended_ref, weight_ref, kept_ref, given_ref, wide, rows):
    seqs, per, depth = attended_ref.shape
    lanes = wide.shape[2]
    for c in range(depth // lanes):
        part = attended_ref[:, :, c * lanes : (c + 1) * lanes].astype(jnp.float32)
        wide[c] = part.reshape(seqs * per, lanes)
        for h in range(per):
            at = h * depth + c * lanes
            rows[:, at : at + lanes] = wide[c, pl.ds(h, seqs, stride=per), :].astype(jnp.bfloat16)
    terms = jnp.dot(rows[...], weight_ref[...], preferred_element_type=jnp.float32)
    own = lax.axis_index("gx")
    size = seqs // halves

    @pl.when(own == 0)
    def _():
        kept_ref[...] = terms[:size]
        given_ref[...] = terms[size:]

    @pl.when(own != 0)
    def _():
        kept_ref[...] = terms[size:]
        given_ref[...] = terms[:size]


def make_on_device(groups, halves):
    swap = [(i, (i + 1) % halves) for i in range(halves)]

    def pairs(k):
        return [(i, i ^ k) for i in range(groups)]

    def on_device(tokens, gain, w_qkv, kv_cache, lengths, w_out):
        f32, bf16 = jnp.float32, jnp.bfloat16
        members = groups * halves
        per, depth = tokens.shape
        width = w_qkv.shape[1]
        wide_out = w_out.shape[1]
        batch = groups * per
        w_in = pltpu.with_memory_space_constraint(w_qkv.T, pltpu.VMEM)
        w_back = pltpu.with_memory_space_constraint(w_out, pltpu.VMEM)

        own, scale, used, spare = call(
            load_kernel,
            [
                jax.ShapeDtypeStruct((per, depth), bf16),
                jax.ShapeDtypeStruct((1, depth), f32),
                jax.ShapeDtypeStruct((8, 128), jnp.int32),
                pltpu.HBM((5 * depth * width // 4096, 1024), bf16),
            ],
            [SMEM, ANY, ANY],
            [pltpu.SemaphoreType.DMA((2,))],
            bytes_of(((8, depth), 8)),
            (per * depth, 2 * per * depth),
            lengths,
            pltpu.with_memory_space_constraint(tokens, pltpu.HBM),
            pltpu.with_memory_space_constraint(gain.reshape(1, -1), pltpu.HBM),
        )
        spare = pltpu.with_memory_space_constraint(spare, pltpu.HBM)
        steps = range(0, groups, 2)
        mates = [own] + [lax.ppermute(tokens, "yz", pairs(k)) for k in steps[1:]]
        column, sums = call(
            column_kernel,
            [
                jax.ShapeDtypeStruct((len(steps), per, depth), bf16),
                jax.ShapeDtypeStruct((len(steps), 2, per, 128), f32),
            ],
            [[VMEM] * len(steps), ANY],
            [],
            bytes_of(((8, depth), 16)),
            (4 * batch * depth, 4 * batch * depth),
            mates,
            spare,
        )
        beside = lax.ppermute(column, "yz", pairs(1))
        other = lax.ppermute(sums, "gx", swap)
        stats = call(
            stats_kernel,
            jax.ShapeDtypeStruct(sums.shape, f32),
            [VMEM, VMEM],
            [],
            bytes_of(((16, 128), 16)),
            (64 * 128, 64 * 128),
            sums,
            other,
        )
        blocks = [column, beside]
        scales = [stats, lax.ppermute(stats, "yz", pairs(1))]
        order = [
            [lambda g, k=k: g ^ k for k in steps],
            [lambda g, k=k: g ^ k ^ 1 for k in steps],
        ]
        parts = call(
            functools.partial(project_kernel, order),
            jax.ShapeDtypeStruct((members, 1, width), f32),
            [[VMEM] * len(blocks), [VMEM] * len(blocks), VMEM, VMEM],
            [
                pltpu.VMEM((batch, depth), f32),
                pltpu.VMEM((2, batch, 128), f32),
                pltpu.VMEM((batch, depth), bf16),
                pltpu.VMEM((batch, width), f32),
            ],
            bytes_of(((batch, depth), 12), ((batch, width + 128), 16), ((BLOCK, BLOCK), 8)),
            (2 * batch * depth * width, depth * width * 2),
            blocks,
            scales,
            scale,
            w_in,
        )
        moved = lax.all_to_all(parts, ("yz", "gx"), 0, 0, tiled=True)
        attended = call(
            functools.partial(attend_kernel, halves),
            jax.ShapeDtypeStruct((members, HQ // halves, HD), bf16),
            [VMEM, VMEM, VMEM, [ANY] * 7],
            [pltpu.VMEM((HQ + 8, HD), f32)],
            bytes_of(((members, HQ // halves, HD), 4), ((512, 512), 4), ((members, 8, width + 128), 8)),
            (4 * HQ * 512 * HD, w_out.shape[0] * wide_out * 2),
            used,
            moved,
            kv_cache,
            [spare] * 7,
        )
        gathered = lax.all_to_all(attended, ("yz", "gx"), 0, 0, tiled=True)
        size = batch // halves
        kept, given = call(
            functools.partial(output_kernel, halves),
            [jax.ShapeDtypeStruct((size, wide_out), f32)] * 2,
            [VMEM, VMEM],
            [
                pltpu.VMEM((HD // 128, batch * (HQ // halves), 128), f32),
                pltpu.VMEM((batch, HQ // halves * HD), bf16),
            ],
            bytes_of(((batch, HQ // halves, HD), 10), ((batch, wide_out + 128), 12)),
            (2 * batch * w_out.shape[0] * wide_out, w_out.shape[0] * wide_out * 2),
            gathered,
            w_back,
        )
        got = lax.ppermute(given, "gx", swap)
        return (kept + got).astype(bf16)

    return on_device


def solution(mesh):
    placed = (
        P(("ga", "yz"), "gx"),
        P("gx"),
        P("gx", "yz"),
        P(("ga", "yz", "gx"), None, None),
        P(("ga", "yz", "gx")),
        P("gx", "yz"),
    )
    return jax.shard_map(
        make_on_device(mesh.shape["yz"], mesh.shape["gx"]),
        mesh=mesh,
        in_specs=placed,
        out_specs=P(("ga", "gx"), "yz"),
        check_vma=False,
    )
```

```python
import functools

import jax
import jax.numpy as jnp
from jax import lax
from jax.experimental import pallas as pl
from jax.experimental.pallas import tpu as pltpu
from jax.sharding import PartitionSpec as P

D = 18432
HQ = 48
HD = 256
BLOCK = 256
MIB = 1 << 20
VMEM = pl.BlockSpec(memory_space=pltpu.VMEM)
SMEM = pl.BlockSpec(memory_space=pltpu.SMEM)
ANY = pl.BlockSpec(memory_space=pl.ANY)


def bytes_of(*shapes):
    total = 0
    for shape, width in shapes:
        size = width
        for dim in shape:
            size *= dim
        total += size
    return total


def spec_of(out):
    return VMEM if isinstance(out, jax.ShapeDtypeStruct) else ANY


def call(kernel, outs, in_specs, scratch, room, cost, *args):
    return pl.pallas_call(
        kernel,
        out_shape=outs,
        in_specs=in_specs,
        out_specs=jax.tree.map(spec_of, outs),
        scratch_shapes=scratch,
        compiler_params=pltpu.CompilerParams(vmem_limit_bytes=room + MIB),
        cost_estimate=pl.CostEstimate(flops=cost[0], bytes_accessed=cost[1], transcendentals=0),
    )(*args)


def load_kernel(
    lengths_ref, tokens_hbm, gain_hbm, own_ref, gain_ref, used_ref, spare_hbm, sems
):
    copies = [
        pltpu.make_async_copy(tokens_hbm, own_ref, sems.at[0]),
        pltpu.make_async_copy(gain_hbm, gain_ref, sems.at[1]),
    ]
    for copy in copies:
        copy.start()
    used_ref[...] = jnp.full(used_ref.shape, lengths_ref[0], jnp.int32)
    for copy in copies:
        copy.wait()


def column_kernel(rows_refs, spare_hbm, column_ref, sums_ref, wide):
    for i, ref in enumerate(rows_refs):
        per = ref.shape[0]
        wide[i * per : (i + 1) * per, :] = ref[...].astype(jnp.float32)
    rows = wide[...]
    column_ref[...] = rows.astype(jnp.bfloat16)
    lanes = sums_ref.shape[1:]
    sums_ref[0] = jnp.broadcast_to(jnp.sum(rows, axis=1, keepdims=True), lanes)
    sums_ref[1] = jnp.broadcast_to(jnp.sum(rows * rows, axis=1, keepdims=True), lanes)


def stats_kernel(sums_ref, other_ref, stats_ref):
    mean = (sums_ref[0] + other_ref[0]) / D
    var = (sums_ref[1] + other_ref[1]) / D - mean * mean
    stats_ref[0] = mean
    stats_ref[1] = lax.rsqrt(var + 1e-06)


def dot_last(left, right):
    return lax.dot_general(
        left, right, (((1,), (1,)), ((), ())), preferred_element_type=jnp.float32
    )


def project_kernel(
    per, order, block_refs, stats_refs, gain_ref, weight_ref, out_ref, rows, terms
):
    group = lax.axis_index("yz")
    places = [origin(group) * per + r for group_of in order for origin in group_of for r in range(per)]
    batch, depth = rows.shape
    width = weight_ref.shape[0]

    def normalise(k):
        cut = slice(k, k + BLOCK)
        parts = []
        for ref, stats_ref in zip(block_refs, stats_refs):
            mean, scale = stats_ref[0][:, 0:1], stats_ref[1][:, 0:1]
            parts.append((ref[:, cut].astype(jnp.float32) - mean) * scale * gain_ref[:, cut])
        rows[:, cut] = jnp.concatenate(parts, axis=0).astype(jnp.bfloat16)

    if width < 2 * BLOCK:
        for k in range(0, depth, BLOCK):
            normalise(k)
    at = 0
    while width - at >= 2 * BLOCK:
        middle, end = at + BLOCK, at + 2 * BLOCK
        first = jnp.zeros((batch, BLOCK), jnp.float32)
        second = jnp.zeros((BLOCK, batch), jnp.float32)
        for k in range(0, depth, BLOCK):
            if at == 0:
                normalise(k)
            some = rows[:, k : k + BLOCK]
            second = second + dot_last(weight_ref[middle:end, k : k + BLOCK], some)
            first = first + dot_last(some, weight_ref[at:middle, k : k + BLOCK])
        terms[:, at:middle] = first
        terms[:, middle:end] = second.T
        at = end
    if at < width:
        terms[:, at:] = dot_last(rows[...], weight_ref[at:, :])
    for i, place in enumerate(places):
        out_ref[place] = terms[i : i + 1, :]


def attend_kernel(halves, used_ref, parts_ref, cache_ref, spare_refs, out_ref, heads):
    width = parts_ref.shape[2]
    pieces = []
    for i in range(parts_ref.shape[0] // halves):
        piece = parts_ref[i * halves]
        for j in range(1, halves):
            piece = piece + parts_ref[i * halves + j]
        pieces.append(piece)
    for h in range(HQ + 2):
        at = 0
        while at < HD:
            where = h * HD + at
            piece, start = where // width, where % width
            size = min(HD - at, width - start)
            heads[h : h + 1, at : at + size] = pieces[piece][:, start : start + size]
            at += size
    query = heads[0:HQ, :].astype(jnp.bfloat16)
    new = heads[HQ : HQ + 2, :].astype(jnp.bfloat16).astype(jnp.float32)
    cache = cache_ref[0]
    scores = (
        lax.dot_general(
            query, cache[:, :HD], (((1,), (1,)), ((), ())), preferred_element_type=jnp.float32
        )
        / 16.0
    )
    score_new = (
        jnp.sum(query.astype(jnp.float32) * new[0:1, :], axis=1, keepdims=True) / 16.0
    )
    valid = lax.broadcasted_iota(jnp.int32, scores.shape, 1) < used_ref[0:1, 0:1]
    masked = jnp.where(valid, scores, -1e30)
    top = jnp.maximum(jnp.max(masked, axis=1, keepdims=True), score_new)
    expd = jnp.where(valid, jnp.exp(masked - top), 0.0)
    exp_new = jnp.exp(score_new - top)
    total = jnp.sum(expd, axis=1, keepdims=True) + exp_new
    probs = (expd / total).astype(jnp.bfloat16)
    prob_new = (exp_new / total).astype(jnp.bfloat16).astype(jnp.float32)
    attended = jnp.dot(probs, cache[:, HD:], preferred_element_type=jnp.float32)
    attended = (attended + prob_new * new[1:2, :]).astype(jnp.bfloat16)
    per = HQ // halves
    for i in range(out_ref.shape[0]):
        j = i % halves
        out_ref[i] = attended[j * per : (j + 1) * per, :]


def output_kernel(halves, attended_ref, weight_ref, kept_ref, given_ref, wide, rows):
    seqs, per, depth = attended_ref.shape
    lanes = wide.shape[2]
    for c in range(depth // lanes):
        part = attended_ref[:, :, c * lanes : (c + 1) * lanes].astype(jnp.float32)
        wide[c] = part.reshape(seqs * per, lanes)
        for h in range(per):
            at = h * depth + c * lanes
            rows[:, at : at + lanes] = wide[c, pl.ds(h, seqs, stride=per), :].astype(jnp.bfloat16)
    terms = jnp.dot(rows[...], weight_ref[...], preferred_element_type=jnp.float32)
    own = lax.axis_index("gx")
    size = seqs // halves

    @pl.when(own == 0)
    def _():
        kept_ref[...] = terms[:size]
        given_ref[...] = terms[size:]

    @pl.when(own != 0)
    def _():
        kept_ref[...] = terms[size:]
        given_ref[...] = terms[:size]


def make_on_device(groups, halves):
    swap = [(i, (i + 1) % halves) for i in range(halves)]

    def pairs(k):
        return [(i, i ^ k) for i in range(groups)]

    def on_device(tokens, gain, w_qkv, kv_cache, lengths, w_out):
        f32, bf16 = jnp.float32, jnp.bfloat16
        members = groups * halves
        per, depth = tokens.shape
        width = w_qkv.shape[1]
        wide_out = w_out.shape[1]
        batch = groups * per
        w_in = pltpu.with_memory_space_constraint(w_qkv.T, pltpu.VMEM)
        w_back = pltpu.with_memory_space_constraint(w_out, pltpu.VMEM)

        own, scale, used, spare = call(
            load_kernel,
            [
                jax.ShapeDtypeStruct((per, depth), bf16),
                jax.ShapeDtypeStruct((1, depth), f32),
                jax.ShapeDtypeStruct((8, 128), jnp.int32),
                pltpu.HBM((5 * depth * width // 4096, 1024), bf16),
            ],
            [SMEM, ANY, ANY],
            [pltpu.SemaphoreType.DMA((2,))],
            bytes_of(((8, depth), 8)),
            (per * depth, 2 * per * depth),
            lengths,
            pltpu.with_memory_space_constraint(tokens, pltpu.HBM),
            pltpu.with_memory_space_constraint(gain.reshape(1, -1), pltpu.HBM),
        )
        spare = pltpu.with_memory_space_constraint(spare, pltpu.HBM)
        steps = range(0, groups, 2)
        mates = [own] + [lax.ppermute(tokens, "yz", pairs(k)) for k in steps[1:]]
        column, sums = call(
            column_kernel,
            [
                jax.ShapeDtypeStruct((batch // 2, depth), bf16),
                jax.ShapeDtypeStruct((2, batch // 2, 128), f32),
            ],
            [[VMEM] * len(steps), ANY],
            [pltpu.VMEM((batch // 2, depth), f32)],
            bytes_of(((8, depth), 8), ((batch, depth), 4)),
            (4 * batch * depth, 4 * batch * depth),
            mates,
            spare,
        )
        beside = lax.ppermute(column, "yz", pairs(1))
        other = lax.ppermute(sums, "gx", swap)
        stats = call(
            stats_kernel,
            jax.ShapeDtypeStruct(sums.shape, f32),
            [VMEM, VMEM],
            [],
            bytes_of(((16, 128), 16)),
            (64 * 128, 64 * 128),
            sums,
            other,
        )
        blocks = [column, beside]
        scales = [stats, lax.ppermute(stats, "yz", pairs(1))]
        order = [
            [lambda g, k=k: g ^ k for k in steps],
            [lambda g, k=k: g ^ k ^ 1 for k in steps],
        ]
        parts = call(
            functools.partial(project_kernel, per, order),
            jax.ShapeDtypeStruct((members, 1, width), f32),
            [[VMEM] * len(blocks), [VMEM] * len(blocks), VMEM, VMEM],
            [
                pltpu.VMEM((batch, depth), bf16),
                pltpu.VMEM((batch, width), f32),
            ],
            bytes_of(((batch, depth), 12), ((batch, width + 128), 16), ((BLOCK, BLOCK), 8)),
            (2 * batch * depth * width, depth * width * 2),
            blocks,
            scales,
            scale,
            w_in,
        )
        moved = lax.all_to_all(parts, ("yz", "gx"), 0, 0, tiled=True)
        attended = call(
            functools.partial(attend_kernel, halves),
            jax.ShapeDtypeStruct((members, HQ // halves, HD), bf16),
            [VMEM, VMEM, VMEM, [ANY] * 7],
            [pltpu.VMEM((HQ + 8, HD), f32)],
            bytes_of(((members, HQ // halves, HD), 4), ((512, 512), 4), ((members, 8, width + 128), 8)),
            (4 * HQ * 512 * HD, w_out.shape[0] * wide_out * 2),
            used,
            moved,
            kv_cache,
            [spare] * 7,
        )
        gathered = lax.all_to_all(attended, ("yz", "gx"), 0, 0, tiled=True)
        size = batch // halves
        kept, given = call(
            functools.partial(output_kernel, halves),
            [jax.ShapeDtypeStruct((size, wide_out), f32)] * 2,
            [VMEM, VMEM],
            [
                pltpu.VMEM((HD // 128, batch * (HQ // halves), 128), f32),
                pltpu.VMEM((batch, HQ // halves * HD), bf16),
            ],
            bytes_of(((batch, HQ // halves, HD), 10), ((batch, wide_out + 128), 12)),
            (2 * batch * w_out.shape[0] * wide_out, w_out.shape[0] * wide_out * 2),
            gathered,
            w_back,
        )
        got = lax.ppermute(given, "gx", swap)
        return (kept + got).astype(bf16)

    return on_device


def solution(mesh):
    placed = (
        P(("ga", "yz"), "gx"),
        P("gx"),
        P("gx", "yz"),
        P(("ga", "yz", "gx"), None, None),
        P(("ga", "yz", "gx")),
        P("gx", "yz"),
    )
    return jax.shard_map(
        make_on_device(mesh.shape["yz"], mesh.shape["gx"]),
        mesh=mesh,
        in_specs=placed,
        out_specs=P(("ga", "gx"), "yz"),
        check_vma=False,
    )
```

```python
import functools

import jax
import jax.numpy as jnp
from jax import lax
from jax.experimental import pallas as pl
from jax.experimental.pallas import tpu as pltpu
from jax.sharding import PartitionSpec as P

D = 18432
HQ = 48
HD = 256
BLOCK = 256
MIB = 1 << 20
VMEM = pl.BlockSpec(memory_space=pltpu.VMEM)
SMEM = pl.BlockSpec(memory_space=pltpu.SMEM)
ANY = pl.BlockSpec(memory_space=pl.ANY)


def bytes_of(*shapes):
    total = 0
    for shape, width in shapes:
        size = width
        for dim in shape:
            size *= dim
        total += size
    return total


def spec_of(out):
    return VMEM if isinstance(out, jax.ShapeDtypeStruct) else ANY


def call(kernel, outs, in_specs, scratch, room, cost, *args):
    return pl.pallas_call(
        kernel,
        out_shape=outs,
        in_specs=in_specs,
        out_specs=jax.tree.map(spec_of, outs),
        scratch_shapes=scratch,
        compiler_params=pltpu.CompilerParams(vmem_limit_bytes=room + MIB),
        cost_estimate=pl.CostEstimate(flops=cost[0], bytes_accessed=cost[1], transcendentals=0),
    )(*args)


def load_kernel(
    lengths_ref, tokens_hbm, gain_hbm, own_ref, gain_ref, used_ref, spare_hbm, sems
):
    copies = [
        pltpu.make_async_copy(tokens_hbm, own_ref, sems.at[0]),
        pltpu.make_async_copy(gain_hbm, gain_ref, sems.at[1]),
    ]
    for copy in copies:
        copy.start()
    used_ref[...] = jnp.full(used_ref.shape, lengths_ref[0], jnp.int32)
    for copy in copies:
        copy.wait()


def column_kernel(rows_refs, spare_hbm, column_ref, sums_ref, wide):
    for i, ref in enumerate(rows_refs):
        per = ref.shape[0]
        wide[i * per : (i + 1) * per, :] = ref[...].astype(jnp.float32)
    rows = wide[...]
    column_ref[...] = rows.astype(jnp.bfloat16)
    lanes = sums_ref.shape[1:]
    sums_ref[0] = jnp.broadcast_to(jnp.sum(rows, axis=1, keepdims=True), lanes)
    sums_ref[1] = jnp.broadcast_to(jnp.sum(rows * rows, axis=1, keepdims=True), lanes)


def stats_kernel(sums_ref, other_ref, stats_ref):
    mean = (sums_ref[0] + other_ref[0]) / D
    var = (sums_ref[1] + other_ref[1]) / D - mean * mean
    stats_ref[0] = mean
    stats_ref[1] = lax.rsqrt(var + 1e-06)


def dot_last(left, right):
    return lax.dot_general(
        left, right, (((1,), (1,)), ((), ())), preferred_element_type=jnp.float32
    )


def project_kernel(block_refs, stats_refs, gain_ref, weight_ref, terms, rows):
    batch, depth = rows.shape
    width = weight_ref.shape[0]

    def normalise(k):
        cut = slice(k, k + BLOCK)
        parts = []
        for ref, stats_ref in zip(block_refs, stats_refs):
            mean, scale = stats_ref[0][:, 0:1], stats_ref[1][:, 0:1]
            parts.append((ref[:, cut].astype(jnp.float32) - mean) * scale * gain_ref[:, cut])
        rows[:, cut] = jnp.concatenate(parts, axis=0).astype(jnp.bfloat16)

    if width < 2 * BLOCK:
        for k in range(0, depth, BLOCK):
            normalise(k)
    at = 0
    while width - at >= 2 * BLOCK:
        middle, end = at + BLOCK, at + 2 * BLOCK
        first = jnp.zeros((batch, BLOCK), jnp.float32)
        second = jnp.zeros((BLOCK, batch), jnp.float32)
        for k in range(0, depth, BLOCK):
            if at == 0:
                normalise(k)
            some = rows[:, k : k + BLOCK]
            second = second + dot_last(weight_ref[middle:end, k : k + BLOCK], some)
            first = first + dot_last(some, weight_ref[at:middle, k : k + BLOCK])
        terms[:, at:middle] = first
        terms[:, middle:end] = second.T
        at = end
    if at < width:
        terms[:, at:] = dot_last(rows[...], weight_ref[at:, :])


def place_kernel(per, order, terms_ref, spare_refs, out_ref):
    group = lax.axis_index("yz")
    places = [origin(group) * per + r for group_of in order for origin in group_of for r in range(per)]
    for i, place in enumerate(places):
        out_ref[place] = terms_ref[i : i + 1, :]


def attend_kernel(halves, used_ref, parts_ref, cache_ref, out_ref, heads):
    width = parts_ref.shape[2]
    pieces = []
    for i in range(parts_ref.shape[0] // halves):
        piece = parts_ref[i * halves]
        for j in range(1, halves):
            piece = piece + parts_ref[i * halves + j]
        pieces.append(piece)
    for h in range(HQ + 2):
        at = 0
        while at < HD:
            where = h * HD + at
            piece, start = where // width, where % width
            size = min(HD - at, width - start)
            heads[h : h + 1, at : at + size] = pieces[piece][:, start : start + size]
            at += size
    query = heads[0:HQ, :].astype(jnp.bfloat16)
    new = heads[HQ : HQ + 2, :].astype(jnp.bfloat16).astype(jnp.float32)
    cache = cache_ref[0]
    scores = (
        lax.dot_general(
            query, cache[:, :HD], (((1,), (1,)), ((), ())), preferred_element_type=jnp.float32
        )
        / 16.0
    )
    score_new = (
        jnp.sum(query.astype(jnp.float32) * new[0:1, :], axis=1, keepdims=True) / 16.0
    )
    valid = lax.broadcasted_iota(jnp.int32, scores.shape, 1) < used_ref[0:1, 0:1]
    masked = jnp.where(valid, scores, -1e30)
    top = jnp.maximum(jnp.max(masked, axis=1, keepdims=True), score_new)
    expd = jnp.where(valid, jnp.exp(masked - top), 0.0)
    exp_new = jnp.exp(score_new - top)
    total = jnp.sum(expd, axis=1, keepdims=True) + exp_new
    probs = (expd / total).astype(jnp.bfloat16)
    prob_new = (exp_new / total).astype(jnp.bfloat16).astype(jnp.float32)
    attended = jnp.dot(probs, cache[:, HD:], preferred_element_type=jnp.float32)
    attended = (attended + prob_new * new[1:2, :]).astype(jnp.bfloat16)
    per = HQ // halves
    for i in range(out_ref.shape[0]):
        j = i % halves
        out_ref[i] = attended[j * per : (j + 1) * per, :]


def output_kernel(halves, attended_ref, weight_ref, kept_ref, given_ref, wide, rows):
    seqs, per, depth = attended_ref.shape
    lanes = wide.shape[2]
    for c in range(depth // lanes):
        part = attended_ref[:, :, c * lanes : (c + 1) * lanes].astype(jnp.float32)
        wide[c] = part.reshape(seqs * per, lanes)
        for h in range(per):
            at = h * depth + c * lanes
            rows[:, at : at + lanes] = wide[c, pl.ds(h, seqs, stride=per), :].astype(jnp.bfloat16)
    terms = jnp.dot(rows[...], weight_ref[...], preferred_element_type=jnp.float32)
    own = lax.axis_index("gx")
    size = seqs // halves

    @pl.when(own == 0)
    def _():
        kept_ref[...] = terms[:size]
        given_ref[...] = terms[size:]

    @pl.when(own != 0)
    def _():
        kept_ref[...] = terms[size:]
        given_ref[...] = terms[:size]


def make_on_device(groups, halves):
    swap = [(i, (i + 1) % halves) for i in range(halves)]

    def pairs(k):
        return [(i, i ^ k) for i in range(groups)]

    def on_device(tokens, gain, w_qkv, kv_cache, lengths, w_out):
        f32, bf16 = jnp.float32, jnp.bfloat16
        members = groups * halves
        per, depth = tokens.shape
        width = w_qkv.shape[1]
        wide_out = w_out.shape[1]
        batch = groups * per
        w_in = pltpu.with_memory_space_constraint(w_qkv.T, pltpu.VMEM)
        w_back = pltpu.with_memory_space_constraint(w_out, pltpu.VMEM)

        own, scale, used, spare = call(
            load_kernel,
            [
                jax.ShapeDtypeStruct((per, depth), bf16),
                jax.ShapeDtypeStruct((1, depth), f32),
                jax.ShapeDtypeStruct((8, 128), jnp.int32),
                pltpu.HBM((5 * depth * width // 4096, 1024), bf16),
            ],
            [SMEM, ANY, ANY],
            [pltpu.SemaphoreType.DMA((2,))],
            bytes_of(((8, depth), 8)),
            (per * depth, 2 * per * depth),
            lengths,
            pltpu.with_memory_space_constraint(tokens, pltpu.HBM),
            pltpu.with_memory_space_constraint(gain.reshape(1, -1), pltpu.HBM),
        )
        spare = pltpu.with_memory_space_constraint(spare, pltpu.HBM)
        steps = range(0, groups, 2)
        mates = [own] + [lax.ppermute(tokens, "yz", pairs(k)) for k in steps[1:]]
        column, sums = call(
            column_kernel,
            [
                jax.ShapeDtypeStruct((batch // 2, depth), bf16),
                jax.ShapeDtypeStruct((2, batch // 2, 128), f32),
            ],
            [[VMEM] * len(steps), ANY],
            [pltpu.VMEM((batch // 2, depth), f32)],
            bytes_of(((8, depth), 8), ((batch, depth), 4)),
            (4 * batch * depth, 4 * batch * depth),
            mates,
            spare,
        )
        beside = lax.ppermute(column, "yz", pairs(1))
        other = lax.ppermute(sums, "gx", swap)
        stats = call(
            stats_kernel,
            jax.ShapeDtypeStruct(sums.shape, f32),
            [VMEM, VMEM],
            [],
            bytes_of(((16, 128), 16)),
            (64 * 128, 64 * 128),
            sums,
            other,
        )
        blocks = [column, beside]
        scales = [stats, lax.ppermute(stats, "yz", pairs(1))]
        order = [
            [lambda g, k=k: g ^ k for k in steps],
            [lambda g, k=k: g ^ k ^ 1 for k in steps],
        ]
        terms = call(
            project_kernel,
            jax.ShapeDtypeStruct((batch, width), f32),
            [[VMEM] * len(blocks), [VMEM] * len(blocks), VMEM, VMEM],
            [
                pltpu.VMEM((batch, depth), bf16),
            ],
            bytes_of(((batch, depth), 12), ((batch, width + 128), 16), ((BLOCK, BLOCK), 8)),
            (2 * batch * depth * width, depth * width * 2),
            blocks,
            scales,
            scale,
            w_in,
        )
        parts = call(
            functools.partial(place_kernel, per, order),
            jax.ShapeDtypeStruct((members, 1, width), f32),
            [VMEM, [ANY] * 7],
            [],
            bytes_of(((batch, width + 128), 16)),
            (batch * width, 8 * batch * width),
            terms,
            [spare] * 7,
        )
        moved = lax.all_to_all(parts, ("yz", "gx"), 0, 0, tiled=True)
        attended = call(
            functools.partial(attend_kernel, halves),
            jax.ShapeDtypeStruct((members, HQ // halves, HD), bf16),
            [VMEM, VMEM, VMEM],
            [pltpu.VMEM((HQ + 8, HD), f32)],
            bytes_of(((members, HQ // halves, HD), 4), ((512, 512), 4), ((members, 8, width + 128), 8)),
            (4 * HQ * 512 * HD, w_out.shape[0] * wide_out * 2),
            used,
            moved,
            kv_cache,
        )
        gathered = lax.all_to_all(attended, ("yz", "gx"), 0, 0, tiled=True)
        size = batch // halves
        kept, given = call(
            functools.partial(output_kernel, halves),
            [jax.ShapeDtypeStruct((size, wide_out), f32)] * 2,
            [VMEM, VMEM],
            [
                pltpu.VMEM((HD // 128, batch * (HQ // halves), 128), f32),
                pltpu.VMEM((batch, HQ // halves * HD), bf16),
            ],
            bytes_of(((batch, HQ // halves, HD), 10), ((batch, wide_out + 128), 12)),
            (2 * batch * w_out.shape[0] * wide_out, w_out.shape[0] * wide_out * 2),
            gathered,
            w_back,
        )
        got = lax.ppermute(given, "gx", swap)
        return (kept + got).astype(bf16)

    return on_device


def solution(mesh):
    placed = (
        P(("ga", "yz"), "gx"),
        P("gx"),
        P("gx", "yz"),
        P(("ga", "yz", "gx"), None, None),
        P(("ga", "yz", "gx")),
        P("gx", "yz"),
    )
    return jax.shard_map(
        make_on_device(mesh.shape["yz"], mesh.shape["gx"]),
        mesh=mesh,
        in_specs=placed,
        out_specs=P(("ga", "gx"), "yz"),
        check_vma=False,
    )
```
